512 devices in a mesh: tile: 16 (over z, core), depth: 32 (over x, y).
Axes of the slice: x: 4, y: 8, z: 8, core: 2. Of those that a mesh axis runs over, the one named last changes fastest.
Arguments:
- density: bfloat16 [512, 512, 1024], P('depth', 'tile'), may hold values from 0.099609375 to 1.5
- materials: int32 [512, 512, 1024], P('depth', 'tile'), may hold values from 0 to 7
- emit_table: float32 [3, 8], replicated, may hold values from 0.001953125 to 0.015625
- absorb_table: float32 [8], replicated, may hold values from 0.0009765625 to 0.0078125
- depth_order: int32 [32], replicated, may hold values from 0 to 31, each once
Outputs:
- colour: float32 [3, 512, 1024], P(None, ('tile', 'depth'))
- opacity: float32 [512, 1024], P(('tile', 'depth'))
The draws below stay inside these ranges and needn't reach their ends.
Inputs may be any that keep to these rules, and one draw needn't show every extreme that they name: depth_order names every slab once.
All inputs are finite; a program needn't handle non-finite values.
Results may differ from the reference program's by a relative error of at most 0.0013.
Values may be sent and summed in bfloat16 or wider, within the bound.
No kernel may reach another device: no remote copies, remote signals or barrier semaphores. Data moves between devices by JAX's collectives and lax.ppermute only.
A program may use at most 64 MiB of HBM per device.

```python
import math
import jax
import jax.numpy as jnp
from jax import lax

Y = 1024
CZ = 16
MAT = 8
X = 512
Z = 512
N_DEPTH = 32


def place_ends(array, rng, least, high):
    spot = [jax.random.randint(jax.random.fold_in(rng, axis), (), 0, length) for axis, length in enumerate(array.shape)]
    widest = array.shape.index(max(array.shape))
    neighbour = spot[:widest] + [(spot[widest] + 1) % array.shape[widest]] + spot[widest + 1:]
    return array.at[tuple(spot)].set(least).at[tuple(neighbour)].set(high)


def steps_of(key, extent, cuts, smallest, top_value):
    def one(position, blocks):
        draws = jax.random.uniform(jax.random.fold_in(jax.random.fold_in(key, 6), position), (blocks,), jnp.float32, smallest / len(cuts), top_value / len(cuts))
        return jnp.repeat(jnp.exp(draws), extent[position] // blocks).reshape((-1,) + (1,) * (len(extent) - position - 1))

    loudness = one(*cuts[0])
    for cut in cuts[1:]:
        loudness = loudness * one(*cut)
    return loudness


def setup_inputs(seed: int = 0) -> dict:
    key_list = jax.random.split(jax.random.key(seed), 6)
    density = jnp.clip(jnp.exp(math.log(1.5) - 2.7119641 * jax.random.uniform(key_list[0], (Z, X, Y), jnp.float32) ** steps_of(key_list[0], (Z, X, Y), ((0, 32), (1, 16)), -0.2, 0.2)), 0.099609375, 1.5).astype(jnp.bfloat16)
    materials = place_ends(jax.random.randint(key_list[1], (Z, X, Y), 0, MAT), jax.random.fold_in(key_list[1], 1), 0, MAT - 1).astype(jnp.int32)
    emit_table = jnp.clip(jnp.exp(jax.random.uniform(key_list[2], (3, MAT), jnp.float32, math.log(0.001953125), math.log(0.015625))), 0.001953125, 0.015625)
    absorb_table = jnp.clip(jnp.exp(jax.random.uniform(key_list[3], (MAT,), jnp.float32, math.log(0.0009765625), math.log(0.0078125))), 0.0009765625, 0.0078125)
    depth_order = jax.random.permutation(key_list[4], N_DEPTH).astype(jnp.int32)
    return {"density": density, "materials": materials, "emit_table": emit_table, "absorb_table": absorb_table, "depth_order": depth_order}


def slab_terms(padded_rows, after_layer, mats, emit_table, absorb_table):
    field = padded_rows[:, 1:-1]
    after = jnp.concatenate([field[1:], after_layer[None]], 0)
    samples = 0.5 * (field + after)
    grad_rows = 0.5 * (padded_rows[:, 2:] - padded_rows[:, :-2])
    padded_cols = jnp.pad(field, ((0, 0), (0, 0), (1, 1)))
    grad_cols = 0.5 * (padded_cols[:, :, 2:] - padded_cols[:, :, :-2])
    shade = 0.6 + 0.4 * jnp.tanh(2.0 * (grad_rows + grad_cols))
    absorb = jnp.zeros_like(field)
    colours = [jnp.zeros_like(field) for channel in range(3)]
    for material in range(MAT):
        hit = mats == material
        absorb = absorb + jnp.where(hit, absorb_table[material], jnp.float32(0.0))
        colours = [colours[channel] + jnp.where(hit, emit_table[channel, material], jnp.float32(0.0)) for channel in range(3)]
    thick = absorb * samples * samples
    inside = jnp.cumsum(thick, 0) - thick
    weight = samples * shade * jnp.exp(-inside)
    image = jnp.stack([jnp.sum(colours[channel] * weight, 0) for channel in range(3)], axis=1)
    return image, jnp.sum(thick, 0)


def reference(density, materials, emit_table, absorb_table, depth_order):
    slabs = N_DEPTH

    def one_slab(slab):
        start = (slab * CZ).astype(jnp.int32)
        dens = lax.dynamic_slice_in_dim(density, start, CZ, 0).astype(jnp.float32)
        mats = lax.dynamic_slice_in_dim(materials, start, CZ, 0)
        later = (jnp.minimum(slab + 1, slabs - 1) * CZ).astype(jnp.int32)
        below = lax.dynamic_index_in_dim(density, later, 0, keepdims=False).astype(jnp.float32)
        below = jnp.where(slab < slabs - 1, below, jnp.float32(0.0))
        padded = jnp.pad(dens, ((0, 0), (1, 1), (0, 0)))
        return slab_terms(padded, below, mats, emit_table, absorb_table)

    images, thicks = lax.map(one_slab, jnp.arange(slabs, dtype=jnp.int32))
    ordered_images = jnp.take(images, depth_order, axis=0)
    ordered_thick = jnp.take(thicks, depth_order, axis=0)
    front = jnp.cumsum(ordered_thick, 0) - ordered_thick
    colour = jnp.sum(ordered_images * jnp.exp(-front)[:, :, None, :], 0)
    opacity = 1.0 - jnp.exp(-jnp.sum(thicks, 0))
    return jnp.transpose(colour, (1, 0, 2)), opacity
```

```python
import functools
import jax
import jax.numpy as jnp
from jax import lax
from jax.experimental import pallas as pl
from jax.experimental.pallas import tpu as pltpu
from jax.sharding import PartitionSpec as P

MAT = 8
LOG2E = 1.4426950408889634
IMAGE_GAIN = 64.0
THICK_GAIN = 128.0


def power16(x):
    x = x * x
    x = x * x
    x = x * x
    return x * x


def root16(x):
    return jnp.exp2(jnp.log2(x) * 0.0625)


def lookup(table, index):
    return jnp.take_along_axis(table, index, axis=1, mode="promise_in_bounds")


def lane_table(read):
    lane = lax.broadcasted_iota(jnp.int32, (8, 128), 1)
    table = jnp.zeros((8, 128), jnp.float32)
    for m in range(MAT):
        table = jnp.where(lane == m, read(m), table)
    return table


def slab_kernel(dens, mats, above, below, after, emit, absorb, out, field, turned):
    cells, rows, cols = dens.shape
    tiles = cols // 128
    for k in range(cells):
        field[k, pl.ds(8, rows), :] = dens[k].astype(jnp.float32)
    field[cells, pl.ds(8, rows), :] = after[...].astype(jnp.float32)
    up = above[...].astype(jnp.float32)
    down = below[...].astype(jnp.float32)
    for k in range(cells):
        field[k, pl.ds(7, 1), :] = up[k : k + 1]
        field[k, pl.ds(8 + rows, 1), :] = down[k : k + 1]
    emits = [lane_table(lambda m, c=c: emit[c, m] * 0.5) for c in range(3)]
    absorbs = lane_table(lambda m: absorb[m] * (0.25 * LOG2E))
    column = lax.broadcasted_iota(jnp.int32, (8, cols), 1)
    first, last = column == 0, column == cols - 1
    for r in range(rows // 8):
        at = 8 + 8 * r

        def layer(k, carry):
            here, inside, red, green, blue = carry
            nxt = field[k + 1, pl.ds(at, 8), :]
            grad = field[k, pl.ds(at + 1, 8), :] - field[k, pl.ds(at - 1, 8), :]
            right = jnp.where(last, 0.0, pltpu.roll(here, cols - 1, 1))
            left = jnp.where(first, 0.0, pltpu.roll(here, 1, 1))
            shade = 0.6 + 0.4 * jnp.tanh(grad + (right - left))
            twice = here + nxt
            weight = twice * shade * jnp.exp2(-inside)
            index = mats[k, pl.ds(8 * r, 8), :]
            pieces = [index[:, 128 * j : 128 * (j + 1)] for j in range(tiles)]
            look = lambda table: jnp.concatenate([lookup(table, p) for p in pieces], 1)
            inside = inside + look(absorbs) * (twice * twice)
            red, green, blue = (
                total + look(table) * weight
                for total, table in zip((red, green, blue), emits)
            )
            return (nxt, inside, red, green, blue)

        zero = jnp.zeros((8, cols), jnp.float32)
        start = (field[0, pl.ds(at, 8), :], zero, zero, zero, zero)
        _, inside, red, green, blue = lax.fori_loop(0, cells, layer, start, unroll=2)
        coded = [power16(v * IMAGE_GAIN) for v in (red, green, blue)]
        coded.append(power16(inside * (THICK_GAIN / LOG2E)))
        for c, value in enumerate(coded):
            for j in range(tiles):
                turned[pl.ds(8 * r * 32 + c * tiles + j, 8, stride=32), :] = value[
                    :, 128 * j : 128 * (j + 1)
                ]
    for i in range(rows):
        out[i] = turned[pl.ds(32 * i, 32), :].astype(jnp.bfloat16)


def final_kernel(order, parts, colour, opacity):
    slabs = parts.shape[0]
    front = jnp.zeros((8, 128), jnp.float32)
    totals = [jnp.zeros((8, 128), jnp.float32) for _ in range(3)]
    for rank in range(slabs):
        slab = order[rank]
        value = root16(parts[slab].astype(jnp.float32))
        through = jnp.exp2(-front)
        for c in range(3):
            totals[c] = totals[c] + value[8 * c : 8 * c + 8] * through
        front = front + value[24:32] * (LOG2E / THICK_GAIN)
    for c in range(3):
        colour[c] = totals[c] * (1.0 / IMAGE_GAIN)
    opacity[...] = 1.0 - jnp.exp2(-front)


def shards(density, materials, emit_table, absorb_table, depth_order):
    cells, rows, cols = density.shape
    tiles, slabs = lax.axis_size("tile"), lax.axis_size("depth")
    up = [(i, i + 1) for i in range(tiles - 1)]
    down = [(i + 1, i) for i in range(tiles - 1)]
    nearer = [(i + 1, i) for i in range(slabs - 1)]
    above = lax.ppermute(density[:, rows - 1], "tile", up)
    below = lax.ppermute(density[:, 0], "tile", down)
    after = lax.ppermute(density[0], "depth", nearer)
    vmem = pl.BlockSpec(memory_space=pltpu.VMEM)
    smem = pl.BlockSpec(memory_space=pltpu.SMEM)
    parts = pl.pallas_call(
        slab_kernel,
        out_shape=jax.ShapeDtypeStruct((rows, 32, 128), jnp.bfloat16),
        in_specs=[vmem] * 5 + [smem] * 2,
        out_specs=vmem,
        scratch_shapes=[
            pltpu.VMEM((cells + 1, rows + 16, cols), jnp.float32),
            pltpu.VMEM((rows * 32, 128), jnp.float32),
        ],
        compiler_params=pltpu.CompilerParams(vmem_limit_bytes=32 << 20),
    )(density, materials, above, below, after, emit_table, absorb_table)
    parts = lax.all_to_all(parts, "depth", 0, 0, tiled=True)
    colour, opacity = pl.pallas_call(
        final_kernel,
        out_shape=(
            jax.ShapeDtypeStruct((3, 8, 128), jnp.float32),
            jax.ShapeDtypeStruct((8, 128), jnp.float32),
        ),
        in_specs=[smem, vmem],
        out_specs=(vmem, vmem),
    )(depth_order, parts)
    return colour.reshape(3, 1, cols), opacity.reshape(1, cols)


def solution(mesh):
    return jax.shard_map(
        shards,
        mesh=mesh,
        in_specs=(P("depth", "tile", None), P("depth", "tile", None), P(), P(), P()),
        out_specs=(P(None, ("tile", "depth"), None), P(("tile", "depth"), None)),
        check_vma=False,
    )
```

```python
import jax
import jax.numpy as jnp
from jax import lax
from jax.experimental import pallas as pl
from jax.experimental.pallas import tpu as pltpu
from jax.sharding import PartitionSpec as P

MAT = 8
LOG2E = 1.4426950408889634
IMAGE_GAIN = 64.0
THICK_GAIN = 128.0
HALF = 4
PITCH = 48


def power16(x):
    x = x * x
    x = x * x
    x = x * x
    return x * x


def root16(x):
    return jnp.exp2(jnp.log2(x) * 0.0625)


def lookup(table, index):
    return jnp.take_along_axis(table, index, axis=0, mode="promise_in_bounds")


def row_table(read):
    row = lax.broadcasted_iota(jnp.int32, (8, 128), 0)
    table = jnp.zeros((8, 128), jnp.float32)
    for m in range(MAT):
        table = jnp.where(row == m, read(m), table)
    return table


def edge_kernel(dens_h, emit_h, absorb_h, dens, layer, near, far, tables, edges, emit, absorb, sems):
    cells, rows, cols = dens.shape
    load = pltpu.make_async_copy(dens_h, dens, sems.at[0])
    load.start()
    load_emit = pltpu.make_async_copy(emit_h, emit, sems.at[1])
    load_emit.start()
    load_absorb = pltpu.make_async_copy(absorb_h, absorb, sems.at[2])
    load_absorb.start()
    load_absorb.wait()
    load_emit.wait()
    tables[0] = row_table(lambda m: absorb[m] * (-0.25 * LOG2E))
    for c in range(3):
        tables[1 + c] = row_table(lambda m, c=c: emit[c, m] * (0.2 * IMAGE_GAIN))
    load.wait()
    layer[...] = dens[0]
    for k in range(cells):
        edges[0, pl.ds(k, 1), :] = dens[k, 0:1, :].astype(jnp.float32)
        edges[1, pl.ds(k, 1), :] = dens[k, rows - 1 : rows, :].astype(jnp.float32)
    odd = lax.axis_index("tile") % 2
    first, last = edges[0], edges[1]
    near[...] = jnp.where(odd == 1, first, last).astype(jnp.bfloat16)
    far[...] = jnp.where(odd == 1, last, first).astype(jnp.bfloat16)


def body_kernel(dens, mats_h, tables, sums, final, border, mats, field, sems):
    cells, rows, cols = dens.shape
    tiles, strips = cols // 128, rows // 8
    loads = []
    for r in range(strips):
        part = pl.ds(8 * r, 8)
        loads.append(pltpu.make_async_copy(mats_h.at[:, part, :], mats.at[:, part, :], sems.at[r]))
        loads[-1].start()
    table = [tables[q] for q in range(4)]
    lane = lax.broadcasted_iota(jnp.int32, (8, 128), 1)
    row = lax.broadcasted_iota(jnp.int32, (8, 128), 0)
    for k in range(cells):
        layer = dens[k].astype(jnp.float32)
        for j in range(tiles):
            field[pl.ds((k * tiles + j) * PITCH + 8, rows), :] = layer[:, 128 * j : 128 * (j + 1)]

    def cell(k, j, at, count=8):
        return field[pl.ds((k * tiles + j) * PITCH + 8 + at, count), :]

    def along(row_number, half, j):
        start = (8 * half * tiles + j) * PITCH + 8 + row_number
        return field[pl.ds(start, 8, stride=tiles * PITCH), :]

    zero = jnp.zeros((8, 128), jnp.float32)

    def across(before, f, behind):
        left = pltpu.roll(jnp.where(lane == 127, before, f), 1, 1)
        right = pltpu.roll(jnp.where(lane == 0, behind, f), 127, 1)
        return right - left

    for r in range(strips):
        loads[r].wait()
        at = 8 * r
        for j0 in range(0, tiles, HALF):
            js = range(j0, j0 + HALF)
            here = [cell(0, j, at) for j in js]
            inside, red, green, blue = ([zero] * HALF for _ in range(4))
            for k in range(cells):
                last = k == cells - 1
                nxt = here if last else [cell(k + 1, j, at) for j in js]
                before = cell(k, j0 - 1, at) if j0 else zero
                behind = cell(k, j0 + HALF, at) if j0 + HALF < tiles else zero
                wide = [before, *here, behind]
                for n, j in enumerate(js):
                    f = here[n]
                    upper, lower = cell(k, j, at - 1), cell(k, j, at + 1)
                    if r == 0:
                        upper = jnp.where(row == 0, 0.0, upper)
                    if r == strips - 1:
                        lower = jnp.where(row == 7, 0.0, lower)
                    shade = 1.5 + jnp.tanh((lower - upper) + across(wide[n], f, wide[n + 2]))
                    index = mats[k, pl.ds(at, 8), 128 * j : 128 * (j + 1)]
                    found = [lookup(t, index) for t in table]
                    spot = pl.ds((r * tiles + j) * 8, 8)
                    if last:
                        for q in range(4):
                            final[q, spot, :] = found[q]
                            sums[q, spot, :] = (inside, red, green, blue)[q][n]
                        final[4, spot, :] = shade * jnp.exp2(inside[n])
                        final[5, spot, :] = f
                        continue
                    twice = f + nxt[n]
                    weight = twice * shade * jnp.exp2(inside[n])
                    inside[n] = inside[n] + found[0] * (twice * twice)
                    red[n] = red[n] + found[1] * weight
                    green[n] = green[n] + found[2] * weight
                    blue[n] = blue[n] + found[3] * weight
                here = nxt

    for e, (own, inner) in enumerate(((0, 1), (rows - 1, rows - 2))):
        sign = 1.0 if e == 0 else -1.0
        f = [[along(own, h, j) for j in range(tiles)] for h in range(2)]
        for j in range(tiles):
            carried = jnp.zeros((1, 128), jnp.float32)
            for h in range(2):
                before = f[h][j - 1] if j else zero
                behind = f[h][j + 1] if j + 1 < tiles else zero
                grad = sign * along(inner, h, j) + across(before, f[h][j], behind)
                behind_first = f[1][j][0:1] if h == 0 else jnp.zeros((1, 128), jnp.float32)
                nxt = pltpu.roll(f[h][j], 7, 0)
                twice = f[h][j] + jnp.where(row == 7, behind_first, nxt)
                index = jnp.concatenate(
                    [mats[8 * h + i, own : own + 1, 128 * j : 128 * (j + 1)] for i in range(8)], 0
                )
                found = [lookup(t, index) for t in table]
                thick = found[0] * twice * twice
                total = thick
                for step in (1, 2, 4):
                    total = total + jnp.where(row >= step, pltpu.roll(total, step, 0), 0.0)
                through = jnp.exp2(total - thick + carried)
                carried = carried + total[7:8]
                spot = (pl.ds(8 * h, 8), pl.ds(128 * j, 128))
                border[e, 0, *spot] = grad
                border[e, 1, *spot] = twice
                for c in range(3):
                    border[e, 2 + c, *spot] = found[1 + c] * through


def join_kernel(sums, final, border, near, far, after, out):
    cells, cols = near.shape
    rows = after.shape[0]
    tiles, strips = cols // 128, rows // 8
    odd = lax.axis_index("tile") % 2
    near_rows, far_rows = near[...].astype(jnp.float32), far[...].astype(jnp.float32)
    up = jnp.where(odd == 1, near_rows, far_rows)
    down = jnp.where(odd == 1, far_rows, near_rows)
    behind = after[...].astype(jnp.float32)
    cell = lax.broadcasted_iota(jnp.int32, (cells, cols), 0)
    row = lax.broadcasted_iota(jnp.int32, (8, 128), 0)
    outer = []
    for e, halo in enumerate((-up, down)):
        own = behind[0:1] if e == 0 else behind[rows - 1 : rows]
        twice = border[e, 1] + jnp.where(cell == cells - 1, own, 0.0)
        weight = twice * (1.5 + jnp.tanh(border[e, 0] + halo))
        outer.append([jnp.sum(border[e, 2 + c] * weight, 0, keepdims=True) for c in range(3)])
    a = lax.broadcasted_iota(jnp.int32, (256, 256), 0)
    b = lax.broadcasted_iota(jnp.int32, (256, 256), 1)
    turn = jnp.where((a // 32 == b % 8) & (a % 32 == b // 8), 1.0, 0.0).astype(jnp.bfloat16)
    stacks = []
    for r in range(strips):
        block = [[None] * tiles for _ in range(4)]
        for j in range(tiles):
            spot = pl.ds((r * tiles + j) * 8, 8)
            part = slice(128 * j, 128 * (j + 1))
            twice = final[5, spot, :] + behind[8 * r : 8 * r + 8, part]
            inside = sums[0, spot, :] + final[0, spot, :] * (twice * twice)
            weight = twice * final[4, spot, :]
            for c in range(3):
                value = sums[1 + c, spot, :] + final[1 + c, spot, :] * weight
                if r == 0:
                    value = jnp.where(row == 0, outer[0][c][:, part], value)
                if r == strips - 1:
                    value = jnp.where(row == 7, outer[1][c][:, part], value)
                block[c][j] = power16(value)
            block[3][j] = power16(inside * (-THICK_GAIN / LOG2E))
        stacks.append(jnp.concatenate([v for c in block for v in c], 0).astype(jnp.bfloat16))
    moved = jnp.dot(turn, jnp.concatenate(stacks, 1), preferred_element_type=jnp.float32)
    for r in range(strips):
        strip = moved[:, 128 * r : 128 * (r + 1)].astype(jnp.bfloat16)
        out[pl.ds(8 * r, 8)] = strip.reshape(8, 32, 128)


def final_kernel(order, parts, colour, opacity):
    slabs = parts.shape[0]
    front = jnp.zeros((8, 128), jnp.float32)
    totals = [jnp.zeros((8, 128), jnp.float32) for _ in range(3)]
    for rank in range(slabs):
        slab = order[rank]
        value = root16(parts[slab].astype(jnp.float32))
        through = jnp.exp2(-front)
        for c in range(3):
            totals[c] = totals[c] + value[8 * c : 8 * c + 8] * through
        front = front + value[24:32] * (LOG2E / THICK_GAIN)
    for c in range(3):
        colour[c] = totals[c] * (1.0 / IMAGE_GAIN)
    opacity[...] = 1.0 - jnp.exp2(-front)


def shards(density, materials, emit_table, absorb_table, depth_order):
    cells, rows, cols = density.shape
    tiles, slabs = lax.axis_size("tile"), lax.axis_size("depth")
    swap = [(i, i ^ 1) for i in range(tiles)]
    cross = [(i, i + 1) for i in range(1, tiles - 1, 2)]
    cross += [(j, i) for i, j in cross]
    nearer = [(i + 1, i) for i in range(slabs - 1)]
    vmem = pl.BlockSpec(memory_space=pltpu.VMEM)
    smem = pl.BlockSpec(memory_space=pltpu.SMEM)
    hbm = pl.BlockSpec(memory_space=pltpu.HBM)
    room = pltpu.CompilerParams(vmem_limit_bytes=32 << 20)
    spots = rows * cols // 128
    dens, layer, near, far, tables = pl.pallas_call(
        edge_kernel,
        out_shape=(
            jax.ShapeDtypeStruct(density.shape, density.dtype),
            jax.ShapeDtypeStruct((rows, cols), density.dtype),
            jax.ShapeDtypeStruct((cells, cols), density.dtype),
            jax.ShapeDtypeStruct((cells, cols), density.dtype),
            jax.ShapeDtypeStruct((4, 8, 128), jnp.float32),
        ),
        in_specs=[hbm] * 3,
        out_specs=(vmem,) * 5,
        scratch_shapes=[
            pltpu.VMEM((2, cells, cols), jnp.float32),
            pltpu.SMEM(emit_table.shape, jnp.float32),
            pltpu.SMEM(absorb_table.shape, jnp.float32),
            pltpu.SemaphoreType.DMA((3,)),
        ],
        compiler_params=room,
    )(density, emit_table, absorb_table)
    after = lax.ppermute(layer, "depth", nearer)
    near = lax.ppermute(near, "tile", swap)
    far = lax.ppermute(far, "tile", cross)
    sums, final, border = pl.pallas_call(
        body_kernel,
        out_shape=(
            jax.ShapeDtypeStruct((4, spots, 128), jnp.float32),
            jax.ShapeDtypeStruct((6, spots, 128), jnp.float32),
            jax.ShapeDtypeStruct((2, 5, cells, cols), jnp.float32),
        ),
        in_specs=[vmem, hbm, vmem],
        out_specs=(vmem,) * 3,
        scratch_shapes=[
            pltpu.VMEM(materials.shape, materials.dtype),
            pltpu.VMEM((cells * (cols // 128) * PITCH, 128), jnp.float32),
            pltpu.SemaphoreType.DMA((rows // 8,)),
        ],
        compiler_params=room,
    )(dens, materials, tables)
    parts = pl.pallas_call(
        join_kernel,
        out_shape=jax.ShapeDtypeStruct((rows, 32, 128), jnp.bfloat16),
        in_specs=[vmem] * 6,
        out_specs=vmem,
        compiler_params=room,
    )(sums, final, border, near, far, after)
    parts = lax.all_to_all(parts, "depth", 0, 0, tiled=True)
    colour, opacity = pl.pallas_call(
        final_kernel,
        out_shape=(
            jax.ShapeDtypeStruct((3, 8, 128), jnp.float32),
            jax.ShapeDtypeStruct((8, 128), jnp.float32),
        ),
        in_specs=[smem, vmem],
        out_specs=(vmem, vmem),
    )(depth_order, parts)
    return colour.reshape(3, 1, cols), opacity.reshape(1, cols)


def solution(mesh):
    return jax.shard_map(
        shards,
        mesh=mesh,
        in_specs=(P("depth", "tile", None), P("depth", "tile", None), P(), P(), P()),
        out_specs=(P(None, ("tile", "depth"), None), P(("tile", "depth"), None)),
        check_vma=False,
    )
```

```python
import jax
import jax.numpy as jnp
from jax import lax
from jax.experimental import pallas as pl
from jax.experimental.pallas import tpu as pltpu
from jax.sharding import PartitionSpec as P

MAT = 8
LOG2E = 1.4426950408889634
IMAGE_GAIN = 64.0
THICK_GAIN = 128.0
HALF = 4
PITCH = 48


def power16(x):
    x = x * x
    x = x * x
    x = x * x
    return x * x


def root16(x):
    return jnp.exp2(jnp.log2(x) * 0.0625)


def lookup(table, index):
    return jnp.take_along_axis(table, index, axis=0, mode="promise_in_bounds")


def row_table(read):
    row = lax.broadcasted_iota(jnp.int32, (8, 128), 0)
    table = jnp.zeros((8, 128), jnp.float32)
    for m in range(MAT):
        table = jnp.where(row == m, read(m), table)
    return table


def edge_kernel(dens_h, mats_h, emit_h, absorb_h, dens, strip, layer, near, far, tables, edges, emit, absorb, sems):
    cells, rows, cols = dens.shape
    load = pltpu.make_async_copy(dens_h, dens, sems.at[0])
    load.start()
    load_mats = pltpu.make_async_copy(mats_h.at[:, pl.ds(0, 8), :], strip, sems.at[3])
    load_mats.start()
    load_emit = pltpu.make_async_copy(emit_h, emit, sems.at[1])
    load_emit.start()
    load_absorb = pltpu.make_async_copy(absorb_h, absorb, sems.at[2])
    load_absorb.start()
    load_absorb.wait()
    load_emit.wait()
    tables[0] = row_table(lambda m: absorb[m] * (-0.25 * LOG2E))
    for c in range(3):
        tables[1 + c] = row_table(lambda m, c=c: emit[c, m] * (0.2 * IMAGE_GAIN))
    load.wait()
    layer[...] = dens[0]
    for k in range(cells):
        edges[0, pl.ds(k, 1), :] = dens[k, 0:1, :].astype(jnp.float32)
        edges[1, pl.ds(k, 1), :] = dens[k, rows - 1 : rows, :].astype(jnp.float32)
    odd = lax.axis_index("tile") % 2
    first, last = edges[0], edges[1]
    near[...] = jnp.where(odd == 1, first, last).astype(jnp.bfloat16)
    far[...] = jnp.where(odd == 1, last, first).astype(jnp.bfloat16)
    load_mats.wait()


def body_kernel(dens, strip, mats_h, tables, sums, final, border, mats, field, sems):
    cells, rows, cols = dens.shape
    tiles, strips = cols // 128, rows // 8
    loads = []
    for r in range(1, strips):
        part = pl.ds(8 * r, 8)
        loads.append(pltpu.make_async_copy(mats_h.at[:, part, :], mats.at[:, part, :], sems.at[r - 1]))
        loads[-1].start()
    table = [tables[q] for q in range(4)]
    lane = lax.broadcasted_iota(jnp.int32, (8, 128), 1)
    row = lax.broadcasted_iota(jnp.int32, (8, 128), 0)
    for k in range(cells):
        layer = dens[k].astype(jnp.float32)
        for j in range(tiles):
            field[pl.ds((k * tiles + j) * PITCH + 8, rows), :] = layer[:, 128 * j : 128 * (j + 1)]

    def cell(k, j, at, count=8):
        return field[pl.ds((k * tiles + j) * PITCH + 8 + at, count), :]

    def along(row_number, half, j):
        start = (8 * half * tiles + j) * PITCH + 8 + row_number
        return field[pl.ds(start, 8, stride=tiles * PITCH), :]

    def pick(k, at, count, j):
        source = strip if at < 8 else mats
        return source[k, pl.ds(at, count), 128 * j : 128 * (j + 1)]

    zero = jnp.zeros((8, 128), jnp.float32)

    def across(before, f, behind):
        left = pltpu.roll(jnp.where(lane == 127, before, f), 1, 1)
        right = pltpu.roll(jnp.where(lane == 0, behind, f), 127, 1)
        return right - left

    for r in range(strips):
        if r:
            loads[r - 1].wait()
        at = 8 * r
        for j0 in range(0, tiles, HALF):
            js = range(j0, j0 + HALF)
            here = [cell(0, j, at) for j in js]
            inside, red, green, blue = ([zero] * HALF for _ in range(4))
            for k in range(cells):
                last = k == cells - 1
                nxt = here if last else [cell(k + 1, j, at) for j in js]
                before = cell(k, j0 - 1, at) if j0 else zero
                behind = cell(k, j0 + HALF, at) if j0 + HALF < tiles else zero
                wide = [before, *here, behind]
                for n, j in enumerate(js):
                    f = here[n]
                    upper, lower = cell(k, j, at - 1), cell(k, j, at + 1)
                    if r == 0:
                        upper = jnp.where(row == 0, 0.0, upper)
                    if r == strips - 1:
                        lower = jnp.where(row == 7, 0.0, lower)
                    shade = 1.5 + jnp.tanh((lower - upper) + across(wide[n], f, wide[n + 2]))
                    index = pick(k, at, 8, j)
                    found = [lookup(t, index) for t in table]
                    spot = pl.ds((r * tiles + j) * 8, 8)
                    if last:
                        for q in range(4):
                            final[q, spot, :] = found[q]
                            sums[q, spot, :] = (inside, red, green, blue)[q][n]
                        final[4, spot, :] = shade * jnp.exp2(inside[n])
                        final[5, spot, :] = f
                        continue
                    twice = f + nxt[n]
                    weight = twice * shade * jnp.exp2(inside[n])
                    inside[n] = inside[n] + found[0] * (twice * twice)
                    red[n] = red[n] + found[1] * weight
                    green[n] = green[n] + found[2] * weight
                    blue[n] = blue[n] + found[3] * weight
                here = nxt

    for e, (own, inner) in enumerate(((0, 1), (rows - 1, rows - 2))):
        sign = 1.0 if e == 0 else -1.0
        f = [[along(own, h, j) for j in range(tiles)] for h in range(2)]
        for j in range(tiles):
            carried = jnp.zeros((1, 128), jnp.float32)
            for h in range(2):
                before = f[h][j - 1] if j else zero
                behind = f[h][j + 1] if j + 1 < tiles else zero
                grad = sign * along(inner, h, j) + across(before, f[h][j], behind)
                behind_first = f[1][j][0:1] if h == 0 else jnp.zeros((1, 128), jnp.float32)
                nxt = pltpu.roll(f[h][j], 7, 0)
                twice = f[h][j] + jnp.where(row == 7, behind_first, nxt)
                index = jnp.concatenate(
                    [pick(8 * h + i, own, 1, j) for i in range(8)], 0
                )
                found = [lookup(t, index) for t in table]
                thick = found[0] * twice * twice
                total = thick
                for step in (1, 2, 4):
                    total = total + jnp.where(row >= step, pltpu.roll(total, step, 0), 0.0)
                through = jnp.exp2(total - thick + carried)
                carried = carried + total[7:8]
                spot = (pl.ds(8 * h, 8), pl.ds(128 * j, 128))
                border[e, 0, *spot] = grad
                border[e, 1, *spot] = twice
                for c in range(3):
                    border[e, 2 + c, *spot] = found[1 + c] * through


def join_kernel(sums, final, border, near, far, after, out):
    cells, cols = near.shape
    rows = after.shape[0]
    tiles, strips = cols // 128, rows // 8
    odd = lax.axis_index("tile") % 2
    near_rows, far_rows = near[...].astype(jnp.float32), far[...].astype(jnp.float32)
    up = jnp.where(odd == 1, near_rows, far_rows)
    down = jnp.where(odd == 1, far_rows, near_rows)
    behind = after[...].astype(jnp.float32)
    cell = lax.broadcasted_iota(jnp.int32, (cells, cols), 0)
    row = lax.broadcasted_iota(jnp.int32, (8, 128), 0)
    outer = []
    for e, halo in enumerate((-up, down)):
        own = behind[0:1] if e == 0 else behind[rows - 1 : rows]
        twice = border[e, 1] + jnp.where(cell == cells - 1, own, 0.0)
        weight = twice * (1.5 + jnp.tanh(border[e, 0] + halo))
        outer.append([jnp.sum(border[e, 2 + c] * weight, 0, keepdims=True) for c in range(3)])
    a = lax.broadcasted_iota(jnp.int32, (256, 256), 0)
    b = lax.broadcasted_iota(jnp.int32, (256, 256), 1)
    turn = jnp.where((a // 32 == b % 8) & (a % 32 == b // 8), 1.0, 0.0).astype(jnp.bfloat16)
    stacks = []
    for r in range(strips):
        block = [[None] * tiles for _ in range(4)]
        for j in range(tiles):
            spot = pl.ds((r * tiles + j) * 8, 8)
            part = slice(128 * j, 128 * (j + 1))
            twice = final[5, spot, :] + behind[8 * r : 8 * r + 8, part]
            inside = sums[0, spot, :] + final[0, spot, :] * (twice * twice)
            weight = twice * final[4, spot, :]
            for c in range(3):
                value = sums[1 + c, spot, :] + final[1 + c, spot, :] * weight
                if r == 0:
                    value = jnp.where(row == 0, outer[0][c][:, part], value)
                if r == strips - 1:
                    value = jnp.where(row == 7, outer[1][c][:, part], value)
                block[c][j] = power16(value)
            block[3][j] = power16(inside * (-THICK_GAIN / LOG2E))
        stacks.append(jnp.concatenate([v for c in block for v in c], 0).astype(jnp.bfloat16))
    moved = jnp.dot(turn, jnp.concatenate(stacks, 1), preferred_element_type=jnp.float32)
    for r in range(strips):
        strip = moved[:, 128 * r : 128 * (r + 1)].astype(jnp.bfloat16)
        out[pl.ds(8 * r, 8)] = strip.reshape(8, 32, 128)


def final_kernel(order, parts, colour, opacity):
    slabs = parts.shape[0]
    front = jnp.zeros((8, 128), jnp.float32)
    totals = [jnp.zeros((8, 128), jnp.float32) for _ in range(3)]
    for rank in range(slabs):
        slab = order[rank]
        value = root16(parts[slab].astype(jnp.float32))
        through = jnp.exp2(-front)
        for c in range(3):
            totals[c] = totals[c] + value[8 * c : 8 * c + 8] * through
        front = front + value[24:32] * (LOG2E / THICK_GAIN)
    for c in range(3):
        colour[c] = totals[c] * (1.0 / IMAGE_GAIN)
    opacity[...] = 1.0 - jnp.exp2(-front)


def shards(density, materials, emit_table, absorb_table, depth_order):
    cells, rows, cols = density.shape
    tiles, slabs = lax.axis_size("tile"), lax.axis_size("depth")
    swap = [(i, i ^ 1) for i in range(tiles)]
    cross = [(i, i + 1) for i in range(1, tiles - 1, 2)]
    cross += [(j, i) for i, j in cross]
    nearer = [(i + 1, i) for i in range(slabs - 1)]
    vmem = pl.BlockSpec(memory_space=pltpu.VMEM)
    smem = pl.BlockSpec(memory_space=pltpu.SMEM)
    hbm = pl.BlockSpec(memory_space=pltpu.HBM)
    density, materials, emit_table, absorb_table = (
        pltpu.with_memory_space_constraint(x, pltpu.HBM)
        for x in (density, materials, emit_table, absorb_table)
    )
    room = pltpu.CompilerParams(vmem_limit_bytes=32 << 20)
    spots = rows * cols // 128
    dens, strip, layer, near, far, tables = pl.pallas_call(
        edge_kernel,
        out_shape=(
            jax.ShapeDtypeStruct(density.shape, density.dtype),
            jax.ShapeDtypeStruct((cells, 8, cols), materials.dtype),
            jax.ShapeDtypeStruct((rows, cols), density.dtype),
            jax.ShapeDtypeStruct((cells, cols), density.dtype),
            jax.ShapeDtypeStruct((cells, cols), density.dtype),
            jax.ShapeDtypeStruct((4, 8, 128), jnp.float32),
        ),
        in_specs=[hbm] * 4,
        out_specs=(vmem,) * 6,
        scratch_shapes=[
            pltpu.VMEM((2, cells, cols), jnp.float32),
            pltpu.SMEM(emit_table.shape, jnp.float32),
            pltpu.SMEM(absorb_table.shape, jnp.float32),
            pltpu.SemaphoreType.DMA((4,)),
        ],
        compiler_params=room,
    )(density, materials, emit_table, absorb_table)
    after = lax.ppermute(layer, "depth", nearer)
    near = lax.ppermute(near, "tile", swap)
    far = lax.ppermute(far, "tile", cross)
    sums, final, border = pl.pallas_call(
        body_kernel,
        out_shape=(
            jax.ShapeDtypeStruct((4, spots, 128), jnp.float32),
            jax.ShapeDtypeStruct((6, spots, 128), jnp.float32),
            jax.ShapeDtypeStruct((2, 5, cells, cols), jnp.float32),
        ),
        in_specs=[vmem, vmem, hbm, vmem],
        out_specs=(vmem,) * 3,
        scratch_shapes=[
            pltpu.VMEM(materials.shape, materials.dtype),
            pltpu.VMEM((cells * (cols // 128) * PITCH, 128), jnp.float32),
            pltpu.SemaphoreType.DMA((rows // 8 - 1,)),
        ],
        compiler_params=room,
    )(dens, strip, materials, tables)
    parts = pl.pallas_call(
        join_kernel,
        out_shape=jax.ShapeDtypeStruct((rows, 32, 128), jnp.bfloat16),
        in_specs=[vmem] * 6,
        out_specs=vmem,
        compiler_params=room,
    )(sums, final, border, near, far, after)
    parts = lax.all_to_all(parts, "depth", 0, 0, tiled=True)
    parts = pltpu.with_memory_space_constraint(parts, pltpu.VMEM)
    colour, opacity = pl.pallas_call(
        final_kernel,
        out_shape=(
            jax.ShapeDtypeStruct((3, 8, 128), jnp.float32),
            jax.ShapeDtypeStruct((8, 128), jnp.float32),
        ),
        in_specs=[smem, vmem],
        out_specs=(vmem, vmem),
    )(depth_order, parts)
    return colour.reshape(3, 1, cols), opacity.reshape(1, cols)


def solution(mesh):
    return jax.shard_map(
        shards,
        mesh=mesh,
        in_specs=(P("depth", "tile", None), P("depth", "tile", None), P(), P(), P()),
        out_specs=(P(None, ("tile", "depth"), None), P(("tile", "depth"), None)),
        check_vma=False,
    )
```

```python
import jax
import jax.numpy as jnp
from jax import lax
from jax.experimental import pallas as pl
from jax.experimental.pallas import tpu as pltpu
from jax.sharding import PartitionSpec as P

MAT = 8
LOG2E = 1.4426950408889634
IMAGE_GAIN = 64.0
THICK_GAIN = 128.0
HALF = 4
PITCH = 48


def power16(x):
    x = x * x
    x = x * x
    x = x * x
    return x * x


def root16(x):
    return jnp.exp2(jnp.log2(x) * 0.0625)


def lookup(table, index):
    return lax.gather(
        table,
        index[..., None],
        lax.GatherDimensionNumbers(
            offset_dims=(),
            collapsed_slice_dims=(0,),
            start_index_map=(0,),
            operand_batching_dims=(1,),
            start_indices_batching_dims=(1,),
        ),
        slice_sizes=(1, 1),
        mode=lax.GatherScatterMode.PROMISE_IN_BOUNDS,
    )


def row_table(read):
    row = lax.broadcasted_iota(jnp.int32, (8, 128), 0)
    table = jnp.zeros((8, 128), jnp.float32)
    for m in range(MAT):
        table = jnp.where(row == m, read(m), table)
    return table


def edge_kernel(dens_h, mats_h, emit_h, absorb_h, dens, strip, layer, near, far, tables, edges, emit, absorb, sems):
    cells, rows, cols = dens.shape
    load = pltpu.make_async_copy(dens_h, dens, sems.at[0])
    load.start()
    load_mats = pltpu.make_async_copy(mats_h.at[:, pl.ds(0, 8), :], strip, sems.at[3])
    load_mats.start()
    load_emit = pltpu.make_async_copy(emit_h, emit, sems.at[1])
    load_emit.start()
    load_absorb = pltpu.make_async_copy(absorb_h, absorb, sems.at[2])
    load_absorb.start()
    load_absorb.wait()
    load_emit.wait()
    tables[0] = row_table(lambda m: absorb[m] * (-0.25 * LOG2E))
    for c in range(3):
        tables[1 + c] = row_table(lambda m, c=c: emit[c, m] * (0.2 * IMAGE_GAIN))
    load.wait()
    layer[...] = dens[0]
    for k in range(cells):
        edges[0, pl.ds(k, 1), :] = dens[k, 0:1, :].astype(jnp.float32)
        edges[1, pl.ds(k, 1), :] = dens[k, rows - 1 : rows, :].astype(jnp.float32)
    odd = lax.axis_index("tile") % 2
    first, last = edges[0], edges[1]
    near[...] = jnp.where(odd == 1, first, last).astype(jnp.bfloat16)
    far[...] = jnp.where(odd == 1, last, first).astype(jnp.bfloat16)
    load_mats.wait()


def body_kernel(dens, strip, mats_h, tables, sums, final, border, mats, field, sems):
    cells, rows, cols = dens.shape
    tiles, strips = cols // 128, rows // 8
    loads = []
    for r in range(1, strips):
        part = pl.ds(8 * r, 8)
        loads.append(pltpu.make_async_copy(mats_h.at[:, part, :], mats.at[:, part, :], sems.at[r - 1]))
        loads[-1].start()
    table = [tables[q] for q in range(4)]
    lane = lax.broadcasted_iota(jnp.int32, (8, 128), 1)
    row = lax.broadcasted_iota(jnp.int32, (8, 128), 0)
    for k in range(cells):
        layer = dens[k].astype(jnp.float32)
        for j in range(tiles):
            field[pl.ds((k * tiles + j) * PITCH + 8, rows), :] = layer[:, 128 * j : 128 * (j + 1)]

    def cell(k, j, at, count=8):
        return field[pl.ds((k * tiles + j) * PITCH + 8 + at, count), :]

    def along(row_number, half, j):
        start = (8 * half * tiles + j) * PITCH + 8 + row_number
        return field[pl.ds(start, 8, stride=tiles * PITCH), :]

    def pick(k, at, count, j):
        source = strip if at < 8 else mats
        return source[k, pl.ds(at, count), 128 * j : 128 * (j + 1)]

    zero = jnp.zeros((8, 128), jnp.float32)

    def across(before, f, behind):
        left = pltpu.roll(jnp.where(lane == 127, before, f), 1, 1)
        right = pltpu.roll(jnp.where(lane == 0, behind, f), 127, 1)
        return right - left

    def edge(e):
        own, inner, sign = ((0, 1, 1.0), (rows - 1, rows - 2, -1.0))[e]
        f = [[along(own, h, j) for j in range(tiles)] for h in range(2)]
        for j in range(tiles):
            carried = jnp.zeros((1, 128), jnp.float32)
            for h in range(2):
                before = f[h][j - 1] if j else zero
                behind = f[h][j + 1] if j + 1 < tiles else zero
                grad = sign * along(inner, h, j) + across(before, f[h][j], behind)
                behind_first = f[1][j][0:1] if h == 0 else jnp.zeros((1, 128), jnp.float32)
                nxt = pltpu.roll(f[h][j], 7, 0)
                twice = f[h][j] + jnp.where(row == 7, behind_first, nxt)
                index = jnp.concatenate(
                    [pick(8 * h + i, own, 1, j) for i in range(8)], 0
                )
                found = [lookup(t, index) for t in table]
                thick = found[0] * twice * twice
                total = thick
                for step in (1, 2, 4):
                    total = total + jnp.where(row >= step, pltpu.roll(total, step, 0), 0.0)
                through = jnp.exp2(total - thick + carried)
                carried = carried + total[7:8]
                spot = (pl.ds(8 * h, 8), pl.ds(128 * j, 128))
                border[e, 0, *spot] = grad
                border[e, 1, *spot] = twice
                for c in range(3):
                    border[e, 2 + c, *spot] = found[1 + c] * through

    for r in range(strips):
        if r == 1:
            edge(0)
        if r:
            loads[r - 1].wait()
        at = 8 * r
        for j0 in range(0, tiles, HALF):
            js = range(j0, j0 + HALF)
            here = [cell(0, j, at) for j in js]
            inside, red, green, blue = ([zero] * HALF for _ in range(4))
            for k in range(cells):
                last = k == cells - 1
                nxt = here if last else [cell(k + 1, j, at) for j in js]
                before = cell(k, j0 - 1, at) if j0 else zero
                behind = cell(k, j0 + HALF, at) if j0 + HALF < tiles else zero
                wide = [before, *here, behind]
                for n, j in enumerate(js):
                    f = here[n]
                    upper, lower = cell(k, j, at - 1), cell(k, j, at + 1)
                    if r == 0:
                        upper = jnp.where(row == 0, 0.0, upper)
                    if r == strips - 1:
                        lower = jnp.where(row == 7, 0.0, lower)
                    shade = 1.5 + jnp.tanh((lower - upper) + across(wide[n], f, wide[n + 2]))
                    index = pick(k, at, 8, j)
                    found = [lookup(t, index) for t in table]
                    spot = pl.ds((r * tiles + j) * 8, 8)
                    if last:
                        for q in range(4):
                            final[q, spot, :] = found[q]
                            sums[q, spot, :] = (inside, red, green, blue)[q][n]
                        final[4, spot, :] = shade * jnp.exp2(inside[n])
                        final[5, spot, :] = f
                        continue
                    twice = f + nxt[n]
                    weight = twice * shade * jnp.exp2(inside[n])
                    inside[n] = inside[n] + found[0] * (twice * twice)
                    red[n] = red[n] + found[1] * weight
                    green[n] = green[n] + found[2] * weight
                    blue[n] = blue[n] + found[3] * weight
                here = nxt
    edge(1)


def join_kernel(sums, final, border, near, far, after, out):
    cells, cols = near.shape
    rows = after.shape[0]
    tiles, strips = cols // 128, rows // 8
    odd = lax.axis_index("tile") % 2
    near_rows, far_rows = near[...].astype(jnp.float32), far[...].astype(jnp.float32)
    up = jnp.where(odd == 1, near_rows, far_rows)
    down = jnp.where(odd == 1, far_rows, near_rows)
    behind = after[...].astype(jnp.float32)
    cell = lax.broadcasted_iota(jnp.int32, (cells, cols), 0)
    row = lax.broadcasted_iota(jnp.int32, (8, 128), 0)
    outer = []
    for e, halo in enumerate((-up, down)):
        own = behind[0:1] if e == 0 else behind[rows - 1 : rows]
        twice = border[e, 1] + jnp.where(cell == cells - 1, own, 0.0)
        weight = twice * (1.5 + jnp.tanh(border[e, 0] + halo))
        outer.append([jnp.sum(border[e, 2 + c] * weight, 0, keepdims=True) for c in range(3)])
    a = lax.broadcasted_iota(jnp.int32, (256, 256), 0)
    b = lax.broadcasted_iota(jnp.int32, (256, 256), 1)
    turn = jnp.where((a // 32 == b % 8) & (a % 32 == b // 8), 1.0, 0.0).astype(jnp.bfloat16)
    stacks = []
    for r in range(strips):
        block = [[None] * tiles for _ in range(4)]
        for j in range(tiles):
            spot = pl.ds((r * tiles + j) * 8, 8)
            part = slice(128 * j, 128 * (j + 1))
            twice = final[5, spot, :] + behind[8 * r : 8 * r + 8, part]
            inside = sums[0, spot, :] + final[0, spot, :] * (twice * twice)
            weight = twice * final[4, spot, :]
            for c in range(3):
                value = sums[1 + c, spot, :] + final[1 + c, spot, :] * weight
                if r == 0:
                    value = jnp.where(row == 0, outer[0][c][:, part], value)
                if r == strips - 1:
                    value = jnp.where(row == 7, outer[1][c][:, part], value)
                block[c][j] = power16(value)
            block[3][j] = power16(inside * (-THICK_GAIN / LOG2E))
        stacks.append(jnp.concatenate([v for c in block for v in c], 0).astype(jnp.bfloat16))
    moved = jnp.dot(turn, jnp.concatenate(stacks, 1), preferred_element_type=jnp.float32)
    for r in range(strips):
        strip = moved[:, 128 * r : 128 * (r + 1)].astype(jnp.bfloat16)
        out[pl.ds(8 * r, 8)] = strip.reshape(8, 32, 128)


def final_kernel(order, parts, colour_h, opacity_h, colour, opacity, sems):
    slabs = parts.shape[0]
    fronts = [jnp.zeros((8, 128), jnp.float32)]
    for rank in range(slabs):
        value = parts[order[rank], 16:32, :].astype(jnp.float32)[8:16]
        fronts.append(fronts[-1] + root16(value) * (-LOG2E / THICK_GAIN))
    opacity[...] = 1.0 - jnp.exp2(fronts[-1])
    send_opacity = pltpu.make_async_copy(opacity, opacity_h, sems.at[0])
    send_opacity.start()
    totals = [jnp.zeros((8, 128), jnp.float32) for _ in range(3)]
    for rank in range(slabs):
        through = jnp.exp2(fronts[rank]) * (1.0 / IMAGE_GAIN)
        value = parts[order[rank]].astype(jnp.float32)
        for c in range(3):
            totals[c] = totals[c] + root16(value[8 * c : 8 * c + 8]) * through
    for c in range(3):
        colour[c] = totals[c]
    send_colour = pltpu.make_async_copy(colour, colour_h, sems.at[1])
    send_colour.start()
    send_opacity.wait()
    send_colour.wait()


def shards(density, materials, emit_table, absorb_table, depth_order):
    cells, rows, cols = density.shape
    tiles, slabs = lax.axis_size("tile"), lax.axis_size("depth")
    swap = [(i, i ^ 1) for i in range(tiles)]
    cross = [(i, i + 1) for i in range(1, tiles - 1, 2)]
    cross += [(j, i) for i, j in cross]
    nearer = [(i + 1, i) for i in range(slabs - 1)]
    vmem = pl.BlockSpec(memory_space=pltpu.VMEM)
    smem = pl.BlockSpec(memory_space=pltpu.SMEM)
    hbm = pl.BlockSpec(memory_space=pltpu.HBM)
    density, materials, emit_table, absorb_table = (
        pltpu.with_memory_space_constraint(x, pltpu.HBM)
        for x in (density, materials, emit_table, absorb_table)
    )
    room = pltpu.CompilerParams(vmem_limit_bytes=32 << 20)
    spots = rows * cols // 128
    dens, strip, layer, near, far, tables = pl.pallas_call(
        edge_kernel,
        out_shape=(
            jax.ShapeDtypeStruct(density.shape, density.dtype),
            jax.ShapeDtypeStruct((cells, 8, cols), materials.dtype),
            jax.ShapeDtypeStruct((rows, cols), density.dtype),
            jax.ShapeDtypeStruct((cells, cols), density.dtype),
            jax.ShapeDtypeStruct((cells, cols), density.dtype),
            jax.ShapeDtypeStruct((4, 8, 128), jnp.float32),
        ),
        in_specs=[hbm] * 4,
        out_specs=(vmem,) * 6,
        scratch_shapes=[
            pltpu.VMEM((2, cells, cols), jnp.float32),
            pltpu.SMEM(emit_table.shape, jnp.float32),
            pltpu.SMEM(absorb_table.shape, jnp.float32),
            pltpu.SemaphoreType.DMA((4,)),
        ],
        compiler_params=room,
    )(density, materials, emit_table, absorb_table)
    after = lax.ppermute(layer, "depth", nearer)
    near = lax.ppermute(near, "tile", swap)
    far = lax.ppermute(far, "tile", cross)
    sums, final, border = pl.pallas_call(
        body_kernel,
        out_shape=(
            jax.ShapeDtypeStruct((4, spots, 128), jnp.float32),
            jax.ShapeDtypeStruct((6, spots, 128), jnp.float32),
            jax.ShapeDtypeStruct((2, 5, cells, cols), jnp.float32),
        ),
        in_specs=[vmem, vmem, hbm, vmem],
        out_specs=(vmem,) * 3,
        scratch_shapes=[
            pltpu.VMEM(materials.shape, materials.dtype),
            pltpu.VMEM(((cells + 1) * (cols // 128) * PITCH, 128), jnp.float32),
            pltpu.SemaphoreType.DMA((rows // 8 - 1,)),
        ],
        compiler_params=room,
    )(dens, strip, materials, tables)
    parts = pl.pallas_call(
        join_kernel,
        out_shape=jax.ShapeDtypeStruct((rows, 32, 128), jnp.bfloat16),
        in_specs=[vmem] * 6,
        out_specs=vmem,
        compiler_params=room,
    )(sums, final, border, near, far, after)
    parts = lax.all_to_all(parts, "depth", 0, 0, tiled=True)
    parts = pltpu.with_memory_space_constraint(parts, pltpu.VMEM)
    colour, opacity = pl.pallas_call(
        final_kernel,
        out_shape=(
            jax.ShapeDtypeStruct((3, 8, 128), jnp.float32),
            jax.ShapeDtypeStruct((8, 128), jnp.float32),
        ),
        in_specs=[smem, vmem],
        out_specs=(hbm, hbm),
        scratch_shapes=[
            pltpu.VMEM((3, 8, 128), jnp.float32),
            pltpu.VMEM((8, 128), jnp.float32),
            pltpu.SemaphoreType.DMA((2,)),
        ],
    )(depth_order, parts)
    return colour.reshape(3, 1, cols), opacity.reshape(1, cols)


def solution(mesh):
    return jax.shard_map(
        shards,
        mesh=mesh,
        in_specs=(P("depth", "tile", None), P("depth", "tile", None), P(), P(), P()),
        out_specs=(P(None, ("tile", "depth"), None), P(("tile", "depth"), None)),
        check_vma=False,
    )
```

```python
import jax
import jax.numpy as jnp
from jax import lax
from jax.experimental import pallas as pl
from jax.experimental.pallas import tpu as pltpu
from jax.sharding import PartitionSpec as P

MAT = 8
LOG2E = 1.4426950408889634
IMAGE_GAIN = 64.0
THICK_GAIN = 128.0
HALF = 4
PITCH = 48


def power16(x):
    x = x * x
    x = x * x
    x = x * x
    return x * x


def root16(x):
    return jnp.exp2(jnp.log2(x) * 0.0625)


def lookup(table, index):
    return lax.gather(
        table,
        index[..., None],
        lax.GatherDimensionNumbers(
            offset_dims=(),
            collapsed_slice_dims=(0,),
            start_index_map=(0,),
            operand_batching_dims=(1,),
            start_indices_batching_dims=(1,),
        ),
        slice_sizes=(1, 1),
        mode=lax.GatherScatterMode.PROMISE_IN_BOUNDS,
    )


def row_table(read):
    row = lax.broadcasted_iota(jnp.int32, (8, 128), 0)
    table = jnp.zeros((8, 128), jnp.float32)
    for m in range(MAT):
        table = jnp.where(row == m, read(m), table)
    return table


def edge_kernel(dens_h, mats_h, emit_h, absorb_h, dens, strip, layer, near, far, tables, turn, edges, emit, absorb, sems):
    cells, rows, cols = dens.shape
    load = pltpu.make_async_copy(dens_h, dens, sems.at[0])
    load.start()
    load_mats = pltpu.make_async_copy(mats_h.at[:, pl.ds(0, 8), :], strip, sems.at[3])
    load_mats.start()
    load_emit = pltpu.make_async_copy(emit_h, emit, sems.at[1])
    load_emit.start()
    load_absorb = pltpu.make_async_copy(absorb_h, absorb, sems.at[2])
    load_absorb.start()
    a = lax.broadcasted_iota(jnp.int32, (256, 256), 0)
    b = lax.broadcasted_iota(jnp.int32, (256, 256), 1)
    turn[...] = jnp.where((a // 32 == b % 8) & (a % 32 == b // 8), 1.0, 0.0).astype(jnp.bfloat16)
    load_absorb.wait()
    load_emit.wait()
    tables[0] = row_table(lambda m: absorb[m] * (-0.25 * LOG2E))
    for c in range(3):
        tables[1 + c] = row_table(lambda m, c=c: emit[c, m] * (0.2 * IMAGE_GAIN))
    load.wait()
    layer[...] = dens[0]
    for k in range(cells):
        edges[0, pl.ds(k, 1), :] = dens[k, 0:1, :].astype(jnp.float32)
        edges[1, pl.ds(k, 1), :] = dens[k, rows - 1 : rows, :].astype(jnp.float32)
    odd = lax.axis_index("tile") % 2
    first, last = edges[0], edges[1]
    near[...] = jnp.where(odd == 1, first, last)
    far[...] = jnp.where(odd == 1, last, first).astype(jnp.bfloat16)
    load_mats.wait()


def body_kernel(dens, strip, mats_h, tables, sums, final, border, mats, field, sems):
    cells, rows, cols = dens.shape
    tiles, strips = cols // 128, rows // 8
    loads = []
    for r in range(1, strips):
        part = pl.ds(8 * r, 8)
        loads.append(pltpu.make_async_copy(mats_h.at[:, part, :], mats.at[:, part, :], sems.at[r - 1]))
        loads[-1].start()
    table = [tables[q] for q in range(4)]
    lane = lax.broadcasted_iota(jnp.int32, (8, 128), 1)
    row = lax.broadcasted_iota(jnp.int32, (8, 128), 0)
    for k in range(cells):
        layer = dens[k].astype(jnp.float32)
        for j in range(tiles):
            field[pl.ds((k * tiles + j) * PITCH + 8, rows), :] = layer[:, 128 * j : 128 * (j + 1)]

    def cell(k, j, at, count=8):
        return field[pl.ds((k * tiles + j) * PITCH + 8 + at, count), :]

    def along(row_number, half, j):
        start = (8 * half * tiles + j) * PITCH + 8 + row_number
        return field[pl.ds(start, 8, stride=tiles * PITCH), :]

    def pick(k, at, count, j):
        source = strip if at < 8 else mats
        return source[k, pl.ds(at, count), 128 * j : 128 * (j + 1)]

    zero = jnp.zeros((8, 128), jnp.float32)

    def across(before, f, behind):
        left = pltpu.roll(jnp.where(lane == 127, before, f), 1, 1)
        right = pltpu.roll(jnp.where(lane == 0, behind, f), 127, 1)
        return right - left

    def edge(e):
        own, inner, sign = ((0, 1, 1.0), (rows - 1, rows - 2, -1.0))[e]
        f = [[along(own, h, j) for j in range(tiles)] for h in range(2)]
        for j in range(tiles):
            carried = jnp.zeros((1, 128), jnp.float32)
            for h in range(2):
                before = f[h][j - 1] if j else zero
                behind = f[h][j + 1] if j + 1 < tiles else zero
                grad = sign * along(inner, h, j) + across(before, f[h][j], behind)
                behind_first = f[1][j][0:1] if h == 0 else jnp.zeros((1, 128), jnp.float32)
                nxt = pltpu.roll(f[h][j], 7, 0)
                twice = f[h][j] + jnp.where(row == 7, behind_first, nxt)
                index = jnp.concatenate(
                    [pick(8 * h + i, own, 1, j) for i in range(8)], 0
                )
                found = [lookup(t, index) for t in table]
                thick = found[0] * twice * twice
                total = thick
                for step in (1, 2, 4):
                    total = total + jnp.where(row >= step, pltpu.roll(total, step, 0), 0.0)
                through = jnp.exp2(total - thick + carried)
                carried = carried + total[7:8]
                spot = (pl.ds(8 * h, 8), pl.ds(128 * j, 128))
                border[e, 0, *spot] = grad
                border[e, 1, *spot] = twice
                for c in range(3):
                    border[e, 2 + c, *spot] = found[1 + c] * through

    for r in range(strips):
        if r == 1:
            edge(0)
        if r:
            loads[r - 1].wait()
        at = 8 * r
        for j0 in range(0, tiles, HALF):
            js = range(j0, j0 + HALF)
            here = [cell(0, j, at) for j in js]
            inside, red, green, blue = ([zero] * HALF for _ in range(4))
            for k in range(cells):
                last = k == cells - 1
                nxt = here if last else [cell(k + 1, j, at) for j in js]
                before = cell(k, j0 - 1, at) if j0 else zero
                behind = cell(k, j0 + HALF, at) if j0 + HALF < tiles else zero
                wide = [before, *here, behind]
                for n, j in enumerate(js):
                    f = here[n]
                    upper, lower = cell(k, j, at - 1), cell(k, j, at + 1)
                    if r == 0:
                        upper = jnp.where(row == 0, 0.0, upper)
                    if r == strips - 1:
                        lower = jnp.where(row == 7, 0.0, lower)
                    shade = 1.5 + jnp.tanh((lower - upper) + across(wide[n], f, wide[n + 2]))
                    index = pick(k, at, 8, j)
                    found = [lookup(t, index) for t in table]
                    spot = pl.ds((r * tiles + j) * 8, 8)
                    if last:
                        for q in range(4):
                            final[q, spot, :] = found[q]
                            sums[q, spot, :] = (inside, red, green, blue)[q][n]
                        final[4, spot, :] = shade * jnp.exp2(inside[n])
                        final[5, spot, :] = f
                        continue
                    twice = f + nxt[n]
                    weight = twice * shade * jnp.exp2(inside[n])
                    inside[n] = inside[n] + found[0] * (twice * twice)
                    red[n] = red[n] + found[1] * weight
                    green[n] = green[n] + found[2] * weight
                    blue[n] = blue[n] + found[3] * weight
                here = nxt
    edge(1)


def join_kernel(sums, final, border, near, after, far, turn, out):
    cells, cols = near.shape
    rows = after.shape[0]
    tiles, strips = cols // 128, rows // 8
    odd = lax.axis_index("tile") % 2
    near_rows, far_rows = near[...].astype(jnp.float32), far[...].astype(jnp.float32)
    up = jnp.where(odd == 1, near_rows, far_rows)
    down = jnp.where(odd == 1, far_rows, near_rows)
    behind = after[...].astype(jnp.float32)
    cell = lax.broadcasted_iota(jnp.int32, (cells, cols), 0)
    row = lax.broadcasted_iota(jnp.int32, (8, 128), 0)
    outer = []
    for e, halo in enumerate((-up, down)):
        own = behind[0:1] if e == 0 else behind[rows - 1 : rows]
        twice = border[e, 1] + jnp.where(cell == cells - 1, own, 0.0)
        weight = twice * (1.5 + jnp.tanh(border[e, 0] + halo))
        outer.append([jnp.sum(border[e, 2 + c] * weight, 0, keepdims=True) for c in range(3)])
    stacks = []
    for r in range(strips):
        block = [[None] * tiles for _ in range(4)]
        for j in range(tiles):
            spot = pl.ds((r * tiles + j) * 8, 8)
            part = slice(128 * j, 128 * (j + 1))
            twice = final[5, spot, :] + behind[8 * r : 8 * r + 8, part]
            inside = sums[0, spot, :] + final[0, spot, :] * (twice * twice)
            weight = twice * final[4, spot, :]
            for c in range(3):
                value = sums[1 + c, spot, :] + final[1 + c, spot, :] * weight
                if r == 0:
                    value = jnp.where(row == 0, outer[0][c][:, part], value)
                if r == strips - 1:
                    value = jnp.where(row == 7, outer[1][c][:, part], value)
                block[c][j] = power16(value)
            block[3][j] = power16(inside * (-THICK_GAIN / LOG2E))
        stacks.append(jnp.concatenate([v for c in block for v in c], 0).astype(jnp.bfloat16))
    moved = jnp.dot(turn[...], jnp.concatenate(stacks, 1), preferred_element_type=jnp.float32)
    for r in range(strips):
        strip = moved[:, 128 * r : 128 * (r + 1)].astype(jnp.bfloat16)
        out[pl.ds(8 * r, 8)] = strip.reshape(8, 32, 128)


def final_kernel(order, parts, colour_h, opacity_h, colour, opacity, sems):
    slabs = parts.shape[0]
    fronts = [jnp.zeros((8, 128), jnp.float32)]
    for rank in range(slabs):
        value = parts[order[rank], 16:32, :].astype(jnp.float32)[8:16]
        fronts.append(fronts[-1] + root16(value) * (-LOG2E / THICK_GAIN))
    opacity[...] = 1.0 - jnp.exp2(fronts[-1])
    send_opacity = pltpu.make_async_copy(opacity, opacity_h, sems.at[0])
    send_opacity.start()
    totals = [jnp.zeros((8, 128), jnp.float32) for _ in range(3)]
    for rank in range(slabs):
        through = jnp.exp2(fronts[rank]) * (1.0 / IMAGE_GAIN)
        value = parts[order[rank]].astype(jnp.float32)
        for c in range(3):
            totals[c] = totals[c] + root16(value[8 * c : 8 * c + 8]) * through
    for c in range(3):
        colour[c] = totals[c]
    send_colour = pltpu.make_async_copy(colour, colour_h, sems.at[1])
    send_colour.start()
    send_opacity.wait()
    send_colour.wait()


def shards(density, materials, emit_table, absorb_table, depth_order):
    cells, rows, cols = density.shape
    tiles, slabs = lax.axis_size("tile"), lax.axis_size("depth")
    swap = [(i, i ^ 1) for i in range(tiles)]
    cross = [(i, i + 1) for i in range(1, tiles - 1, 2)]
    cross += [(j, i) for i, j in cross]
    nearer = [(i + 1, i) for i in range(slabs - 1)]
    vmem = pl.BlockSpec(memory_space=pltpu.VMEM)
    smem = pl.BlockSpec(memory_space=pltpu.SMEM)
    hbm = pl.BlockSpec(memory_space=pltpu.HBM)
    density, materials, emit_table, absorb_table = (
        pltpu.with_memory_space_constraint(x, pltpu.HBM)
        for x in (density, materials, emit_table, absorb_table)
    )
    room = pltpu.CompilerParams(vmem_limit_bytes=32 << 20)
    spots = rows * cols // 128
    dens, strip, layer, near, far, tables, turn = pl.pallas_call(
        edge_kernel,
        out_shape=(
            jax.ShapeDtypeStruct(density.shape, density.dtype),
            jax.ShapeDtypeStruct((cells, 8, cols), materials.dtype),
            jax.ShapeDtypeStruct((rows, cols), density.dtype),
            jax.ShapeDtypeStruct((cells, cols), jnp.float32),
            jax.ShapeDtypeStruct((cells, cols), density.dtype),
            jax.ShapeDtypeStruct((4, 8, 128), jnp.float32),
            jax.ShapeDtypeStruct((256, 256), jnp.bfloat16),
        ),
        in_specs=[hbm] * 4,
        out_specs=(vmem,) * 7,
        scratch_shapes=[
            pltpu.VMEM((2, cells, cols), jnp.float32),
            pltpu.SMEM(emit_table.shape, jnp.float32),
            pltpu.SMEM(absorb_table.shape, jnp.float32),
            pltpu.SemaphoreType.DMA((4,)),
        ],
        compiler_params=room,
    )(density, materials, emit_table, absorb_table)
    after = lax.ppermute(layer, "depth", nearer)
    near = lax.ppermute(near, "tile", swap)
    far = lax.ppermute(far, "tile", cross)
    sums, final, border = pl.pallas_call(
        body_kernel,
        out_shape=(
            jax.ShapeDtypeStruct((4, spots, 128), jnp.float32),
            jax.ShapeDtypeStruct((6, spots, 128), jnp.float32),
            jax.ShapeDtypeStruct((2, 5, cells, cols), jnp.float32),
        ),
        in_specs=[vmem, vmem, hbm, vmem],
        out_specs=(vmem,) * 3,
        scratch_shapes=[
            pltpu.VMEM(materials.shape, materials.dtype),
            pltpu.VMEM(((cells + 1) * (cols // 128) * PITCH, 128), jnp.float32),
            pltpu.SemaphoreType.DMA((rows // 8 - 1,)),
        ],
        compiler_params=room,
    )(dens, strip, materials, tables)
    parts = pl.pallas_call(
        join_kernel,
        out_shape=jax.ShapeDtypeStruct((rows, 32, 128), jnp.bfloat16),
        in_specs=[vmem] * 7,
        out_specs=vmem,
        compiler_params=room,
    )(sums, final, border, near, after, far, turn)
    parts = lax.all_to_all(parts, "depth", 0, 0, tiled=True)
    parts = pltpu.with_memory_space_constraint(parts, pltpu.VMEM)
    colour, opacity = pl.pallas_call(
        final_kernel,
        out_shape=(
            jax.ShapeDtypeStruct((3, 8, 128), jnp.float32),
            jax.ShapeDtypeStruct((8, 128), jnp.float32),
        ),
        in_specs=[smem, vmem],
        out_specs=(hbm, hbm),
        scratch_shapes=[
            pltpu.VMEM((3, 8, 128), jnp.float32),
            pltpu.VMEM((8, 128), jnp.float32),
            pltpu.SemaphoreType.DMA((2,)),
        ],
    )(depth_order, parts)
    return colour.reshape(3, 1, cols), opacity.reshape(1, cols)


def solution(mesh):
    return jax.shard_map(
        shards,
        mesh=mesh,
        in_specs=(P("depth", "tile", None), P("depth", "tile", None), P(), P(), P()),
        out_specs=(P(None, ("tile", "depth"), None), P(("tile", "depth"), None)),
        check_vma=False,
    )
```
